32 devices in a mesh: row: 8 (over y, x, core), col: 4 (over z).
Axes of the slice: x: 2, y: 2, z: 4, core: 2. Of those that a mesh axis runs over, the one named last changes fastest.
Arguments:
- positions: bfloat16 [3, 49152], P(None, 'row'), may hold values from -3.3 to 3.3, as said below
- normals: bfloat16 [3, 49152], P(None, 'row'), may hold values from -1 to 1, as said below
- areas: bfloat16 [49152], P('row'), as said below
- radiosity: bfloat16 [32, 49152], P(None, 'row'), may hold values from 0.19921875 to 5
- reflect: float32 [49152], P('row'), may hold values from 0.2 to 0.9
- partial_sums: float32 [128, 49152], P('col', 'row'), may hold values from -6 to 6
- visible: int32 [384, 384], P('row'), may hold values 0 or 1
- section: int32 [1], replicated, may hold values from 0 to 7
Outputs:
- advanced: float32 [128, 49152], P('col', 'row')
The draws below stay inside these ranges and needn't reach their ends.
Inputs may be any that keep to these rules, and one draw needn't show every extreme that they name: `positions`: patches of one block lie around a common centre. `normals`: each column has length close to 1. `areas`: each area is positive; 6144 times an area lies between 51 and 1640.
All inputs are finite; a program needn't handle non-finite values. No bound on the sum of `visible` on one device may be relied on, other than what follows from the above.
Results may differ from the reference program's by a relative error of at most 0.0003.
Values may be sent and summed in bfloat16 or wider, within the bound.
No kernel may reach another device: no remote copies, remote signals or barrier semaphores. Data moves between devices by JAX's collectives and lax.ppermute only.
A program may use at most 64 MiB of HBM per device.

```python
import math
import jax
import jax.numpy as jnp
from jax import lax

NB = 6144
CASES = 32
N = 49152
N_ROW = 8
N_COL = 4


def draw_positions(key, part):
    key = jax.random.fold_in(key, 11)
    center_key, local_key = jax.random.split(key)
    centers = jax.random.uniform(center_key, (3, N // NB), jnp.float32, -1.5, 1.5)
    local = jax.random.uniform(local_key, (3, N), jnp.float32, -1.0, 1.0)
    return (jnp.repeat(centers, NB, axis=1) + local).astype(jnp.bfloat16)


def draw_normals(key, part):
    key = jax.random.fold_in(key, 23)
    height_key, angle_key = jax.random.split(key)
    height = jax.random.uniform(height_key, (N,), jnp.float32, -1.0, 1.0)
    angle = jax.random.uniform(angle_key, (N,), jnp.float32, -3.14159265, 3.14159265)
    radius = jnp.sqrt(jnp.maximum(1.0 - height * height, 0.0))
    return jnp.stack([radius * jnp.cos(angle), radius * jnp.sin(angle), height], axis=0).astype(jnp.bfloat16)


def draw_areas(key, part):
    key = jax.random.fold_in(key, 37)
    low, high = (100.0, 800.0)
    level = jax.random.uniform(key, (N,), jnp.float32, jnp.log(low), jnp.log(high))
    return (jnp.exp(level) / NB).astype(jnp.bfloat16)


def touch_ends(array, key, smallest, high):
    longest = array.shape.index(max(array.shape))
    spots = []
    for shift in (0, 1):
        where = [jax.random.randint(jax.random.fold_in(key, axis), (), 0, length) for axis, length in enumerate(array.shape)]
        where[longest] = (where[longest] + shift) % array.shape[longest]
        spots.append(tuple(where))
    return array.at[spots[0]].set(smallest).at[spots[1]].set(high)


def shard_levels(rng, dims, cuts, least, high):
    level, own = 1.0, jax.random.fold_in(rng, 6)
    for position, blocks in cuts:
        steps = jnp.exp(jax.random.uniform(jax.random.fold_in(own, position), (blocks,), jnp.float32, least / len(cuts), high / len(cuts)))
        level = level * jnp.repeat(steps, dims[position] // blocks).reshape([-1 if axis == position else 1 for axis in range(len(dims))])
    return level


def centred(stream_key, shape, spread, limit, shards=(), kind=jnp.bfloat16):
    loudness = shard_levels(stream_key, shape, shards, -0.22, 0.18) if shards else 1.0
    drawn = jax.random.normal(stream_key, shape, jnp.float32) * spread * loudness
    return jnp.minimum(jnp.maximum(drawn, -limit), limit).astype(kind)


def setup_inputs(seed: int = 0) -> dict:
    splits = jax.random.split(jax.random.key(seed), 9)
    return {
        "positions": draw_positions(jax.random.fold_in(splits[8], 71), 0),
        "normals": draw_normals(jax.random.fold_in(splits[8], 71), 0),
        "areas": draw_areas(jax.random.fold_in(splits[8], 71), 0),
        "radiosity": jnp.clip(jnp.exp(math.log(5.0) - 3.2227897 * jax.random.uniform(splits[3], (CASES, N), jnp.float32) ** shard_levels(splits[3], (CASES, N), ((1, 8),), -0.2, 0.2)), 0.19921875, 5.0).astype(jnp.bfloat16),
        "reflect": jnp.clip(0.2 + 0.7 * jax.random.uniform(splits[4], (N,), jnp.float32) ** shard_levels(splits[4], (N,), ((0, 8),), -0.2, 0.2), 0.2, 0.9),
        "partial_sums": centred(splits[5], (N_COL * CASES, N), 1.0, 6.0, ((0, 4), (1, 8)), jnp.float32),
        "visible": touch_ends((jax.random.randint(splits[6], (N // 128, N // 128), 0, 4) < 3).astype(jnp.int32), jax.random.fold_in(splits[6], 1), 0, 1),
        "section": jax.random.randint(splits[7], (1,), 0, N_ROW).astype(jnp.int32),
    }


def block_term(rec_pos, rec_nrm, em_pos, em_nrm, em_area, em_rad, mask_block):
    rows = rec_pos.shape[1]
    cols = em_pos.shape[1]
    row_block_size = min(1024, rows)
    column_block_size = min(2048, cols)
    rcount = rows // row_block_size
    ccount = cols // column_block_size
    cases = em_rad.shape[0]

    def one_block(index):
        start = index * row_block_size
        rpos = lax.dynamic_slice_in_dim(rec_pos, start, row_block_size, 1).astype(jnp.float32)
        rnrm = lax.dynamic_slice_in_dim(rec_nrm, start, row_block_size, 1).astype(jnp.float32)
        matrix_row_count = lax.dynamic_slice_in_dim(mask_block, index * (row_block_size // 128), row_block_size // 128, 0)

        def one_column(total, column_block_index):
            cstart = column_block_index * column_block_size
            epos = lax.dynamic_slice_in_dim(em_pos, cstart, column_block_size, 1).astype(jnp.float32)
            enrm = lax.dynamic_slice_in_dim(em_nrm, cstart, column_block_size, 1).astype(jnp.float32)
            earea = lax.dynamic_slice_in_dim(em_area, cstart, column_block_size, 0).astype(jnp.float32)
            erad = lax.dynamic_slice_in_dim(em_rad, cstart, column_block_size, 1)
            matrix_tile_block = lax.dynamic_slice_in_dim(matrix_row_count, column_block_index * (column_block_size // 128), column_block_size // 128, 1)
            delta_x = rpos[0][:, None] - epos[0][None, :]
            delta_y = rpos[1][:, None] - epos[1][None, :]
            delta_z = rpos[2][:, None] - epos[2][None, :]
            dist_sq = delta_x * delta_x + delta_y * delta_y + delta_z * delta_z
            emit_cos = jnp.maximum(enrm[0][None, :] * delta_x + enrm[1][None, :] * delta_y + enrm[2][None, :] * delta_z, 0.0)
            recv_cos = jnp.maximum(-(rnrm[0][:, None] * delta_x + rnrm[1][:, None] * delta_y + rnrm[2][:, None] * delta_z), 0.0)
            kernel = emit_cos * recv_cos * earea[None, :] / ((dist_sq + earea[None, :]) * (math.pi * dist_sq + earea[None, :]))
            receiver_tile_count = matrix_tile_block.shape[0]
            emitter_tile_count = matrix_tile_block.shape[1]
            visited_flags = jnp.broadcast_to(matrix_tile_block[:, None, :, None], (receiver_tile_count, 128, emitter_tile_count, 128)).reshape(row_block_size, column_block_size)
            view = (kernel * visited_flags.astype(jnp.float32)).astype(jnp.bfloat16)
            return total + jnp.dot(erad, view.T, preferred_element_type=jnp.float32), None

        init = jnp.zeros((cases, row_block_size), jnp.float32)
        total, unused = lax.scan(one_column, init, jnp.arange(ccount, dtype=jnp.int32))
        return total

    parts = lax.map(one_block, jnp.arange(rcount, dtype=jnp.int32))
    return jnp.transpose(parts, (1, 0, 2)).reshape(cases, rows)


def reference(positions, normals, areas, radiosity, reflect, partial_sums, visible, section):
    tiles = NB // 128

    def per_column(column):
        emit = ((column + section[0]) % N_ROW).astype(jnp.int32)
        estart = (emit * NB).astype(jnp.int32)
        em_pos = lax.dynamic_slice_in_dim(positions, estart, NB, 1)
        em_nrm = lax.dynamic_slice_in_dim(normals, estart, NB, 1)
        em_area = lax.dynamic_slice_in_dim(areas, estart, NB, 0)
        em_rad = lax.dynamic_slice_in_dim(radiosity, estart, NB, 1)
        mask_cols = lax.dynamic_slice_in_dim(visible, (emit * tiles).astype(jnp.int32), tiles, 1)

        def per_row(block):
            rstart = (block * NB).astype(jnp.int32)
            rec_pos = lax.dynamic_slice_in_dim(positions, rstart, NB, 1)
            rec_nrm = lax.dynamic_slice_in_dim(normals, rstart, NB, 1)
            mask_block = lax.dynamic_slice_in_dim(mask_cols, (block * tiles).astype(jnp.int32), tiles, 0)
            return block_term(rec_pos, rec_nrm, em_pos, em_nrm, em_area, em_rad, mask_block)

        terms = lax.map(per_row, jnp.arange(N_ROW, dtype=jnp.int32))
        terms = jnp.transpose(terms, (1, 0, 2)).reshape(CASES, N)
        previous = ((column - 1) % N_COL).astype(jnp.int32)
        carried = lax.dynamic_slice_in_dim(partial_sums, (previous * CASES).astype(jnp.int32), CASES, 0)
        return carried + reflect[None, :] * terms

    slots = lax.map(per_column, jnp.arange(N_COL, dtype=jnp.int32))
    return slots.reshape(N_COL * CASES, N)
```

```python
import functools
import math

import jax
import jax.numpy as jnp
from jax import lax
from jax.experimental import pallas as pl
from jax.experimental.pallas import tpu as pltpu
from jax.sharding import PartitionSpec as P

BF = jnp.bfloat16
F32 = jnp.float32
TILE = 128
FEATURES = 32
BITS = 6
GROUP = 4
STEP = 4
MATMUL_COS = 2
KAPPA = (math.pi - 1) / (2 * math.pi)
SIGMA = (math.pi + 1) / (2 * math.pi)


def split3(x):
    high = lax.reduce_precision(x, 8, 7)
    rest = x - high
    mid = lax.reduce_precision(rest, 8, 7)
    return high.astype(BF), mid.astype(BF), (rest - mid).astype(BF)


def filled(rows):
    return rows + [jnp.zeros_like(rows[0])] * (FEATURES - len(rows))


def receiver_features(pos, nrm):
    p, n = pos.astype(F32), nrm.astype(F32)
    square = split3(p[0] * p[0] + p[1] * p[1] + p[2] * p[2])
    own = split3(-(n[0] * p[0] + n[1] * p[1] + n[2] * p[2]))
    one = jnp.ones_like(pos[0])
    rows = [pos[i] for i in range(3) for _ in range(3)]
    rows += [square[i] for i in (0, 0, 1, 1, 0, 2)] + [one] * 3
    rows += [nrm[0], nrm[1], nrm[2], *own]
    return jnp.stack(filled(rows), 0).reshape(FEATURES, -1, TILE).transpose(1, 2, 0)


def emitter_features(pos, nrm, area):
    p, n, a = pos.astype(F32), nrm.astype(F32), area.astype(F32)
    scale = 1.0 / (KAPPA * a)
    gain = 1.0 / (math.pi * KAPPA * KAPPA * a)
    one, zero = jnp.ones_like(pos[0]), jnp.zeros_like(pos[0])
    s = split3(scale)
    t = split3(scale * (p[0] * p[0] + p[1] * p[1] + p[2] * p[2]) + SIGMA / KAPPA)
    e = [gain * n[0], gain * n[1], gain * n[2]]
    e.append(-(e[0] * p[0] + e[1] * p[1] + e[2] * p[2]))
    width = [x for i in range(3) for x in split3(-2.0 * scale * p[i])]
    width += [s[i] for i in (0, 1, 0, 1, 2, 0)] + list(t)
    receive = [zero] * 18 + [pos[0], pos[1], pos[2], one, one, one]
    emit = [x for i in range(3) for x in split3(e[i])] + [zero] * 6 + list(split3(e[3]))
    f = jnp.stack([jnp.stack(filled(r), 0) for r in (width, receive, emit)], 0)
    f = f.reshape(3, FEATURES, -1, TILE).transpose(2, 1, 0, 3)
    f = f.reshape(-1, FEATURES, 3 * TILE)
    f = jnp.concatenate([f, jnp.zeros_like(f[:1])], 0)
    e = jnp.stack(e + [jnp.zeros_like(e[0])] * 4, 0).reshape(8, -1, TILE).transpose(1, 0, 2)
    return f, jnp.concatenate([e, jnp.zeros_like(e[:1])], 0)


def visible_groups(mask):
    n_rec, n_em = mask.shape
    cum = jnp.cumsum(mask, axis=1)
    groups = (cum[:, -1] + GROUP - 1) // GROUP
    ends = jnp.cumsum(groups)
    length = n_rec * ((n_em + GROUP - 1) // GROUP) + 2 * STEP
    q = jnp.arange(length, dtype=jnp.int32)
    a = jnp.sum((ends[None, :] <= q[:, None]).astype(jnp.int32), axis=1)
    hot = a[:, None] == jnp.arange(n_rec, dtype=jnp.int32)[None, :]
    rows = jnp.dot(hot.astype(F32), cum.astype(F32), preferred_element_type=F32)
    first = jnp.sum(jnp.where(hot, (ends - groups)[None, :], 0), axis=1)
    rank = (GROUP * (q - first)).astype(F32)
    code = jnp.minimum(a, n_rec - 1)
    for t in range(GROUP):
        code = (code << BITS) + jnp.sum((rows <= rank[:, None] + t).astype(jnp.int32), axis=1)
    return ends[-1:], code


def decoded(code):
    last = (1 << BITS) - 1
    return code >> (BITS * GROUP), [
        (code >> (BITS * (GROUP - 1 - t))) & last for t in range(GROUP)
    ]


def term_kernel(count, codes, rec, em, emit_rows, rad, out, place, view):
    steps = (count[0] + STEP - 1) // STEP
    out[...] = jnp.zeros_like(out)
    view[...] = jnp.zeros_like(view)

    row = lax.broadcasted_iota(jnp.int32, (FEATURES, 3 * TILE), 0)
    col = lax.broadcasted_iota(jnp.int32, (FEATURES, 3 * TILE), 1)
    chosen = jnp.where(row == 3 * (col // TILE), 1.0, 0.0).astype(BF)

    def spread(a, carry):
        spreaded = jnp.dot(rec[a], chosen, preferred_element_type=F32)
        for i in range(3):
            place[a, i] = spreaded[:, i * TILE : (i + 1) * TILE]
        return carry

    lax.fori_loop(0, rec.shape[0], spread, 0, unroll=4)

    def views(a, tiles, slot):
        products = [
            jnp.dot(
                rec[a],
                em[b] if t < MATMUL_COS else em[b, :, : 2 * TILE],
                preferred_element_type=F32,
            )
            for t, b in enumerate(tiles)
        ]
        for r in range(0, TILE, 32):
            x, y, z = (place[a, i, r : r + 32] for i in range(3))
            for t, b in enumerate(tiles):
                m = products[t][r : r + 32]
                if t < MATMUL_COS:
                    cos = m[:, 2 * TILE :]
                else:
                    e = [emit_rows[b, i : i + 1] for i in range(4)]
                    cos = e[0] * x + e[1] * y + e[2] * z + e[3]
                w = m[:, :TILE]
                v = jnp.maximum(cos, 0.0) * m[:, TILE : 2 * TILE]
                v = v * pltpu.reciprocal(w * w - 1.0, approx=True)
                view[slot, r : r + 32, t * TILE : (t + 1) * TILE] = jnp.maximum(v.astype(BF), 0)

    def add(a, tiles, slot):
        r = jnp.concatenate([rad[b] for b in tiles], axis=1)
        at = pl.ds(pl.multiple_of(a * TILE, TILE), TILE)
        out[:, at] += lax.dot_general(
            r, view[slot], (((1,), (1,)), ((), ())), preferred_element_type=F32
        )

    def step(i, carry):
        for j in range(STEP):
            add(*decoded(codes[jnp.maximum(i - 1, 0) * STEP + j]), j)
            views(*decoded(codes[i * STEP + j]), j)
        return carry

    lax.fori_loop(0, steps + 1, step, 0)


def block_term(count, codes, rec, em, emit_rows, rad):
    tiles, cases = rec.shape[0], rad.shape[1]
    smem = pl.BlockSpec(memory_space=pltpu.SMEM)
    vmem = pl.BlockSpec(memory_space=pltpu.VMEM)
    pairs = tiles * tiles * TILE * TILE
    return pl.pallas_call(
        term_kernel,
        out_shape=jax.ShapeDtypeStruct((cases, tiles * TILE), F32),
        in_specs=[smem] * 2 + [vmem] * 4,
        out_specs=vmem,
        scratch_shapes=[
            pltpu.VMEM((tiles, 3, TILE, TILE), F32),
            pltpu.VMEM((STEP, TILE, GROUP * TILE), BF),
        ],
        compiler_params=pltpu.CompilerParams(vmem_limit_bytes=56 * 2**20),
        cost_estimate=pl.CostEstimate(
            flops=pairs * 200, bytes_accessed=8 * 2**20, transcendentals=pairs
        ),
        name="block_term",
    )(count, codes, rec, em, emit_rows, rad)


def from_root(block, axis, root):
    n = lax.axis_size(axis)
    me = lax.axis_index(axis)
    bit = 1
    while bit < n:
        got = lax.ppermute(block, axis, [(i, i ^ bit) for i in range(n)])
        block = jnp.where((me & bit) == (root & bit), block, got)
        bit *= 2
    return block


def shifted(block, axis, distance):
    n = lax.axis_size(axis)
    return lax.ppermute(block, axis, [((i - distance) % n, i) for i in range(n)])


def on_device(positions, normals, areas, radiosity, reflect, partial_sums, visible, section):
    carried = shifted(partial_sums, "col", 1)
    n_row = lax.axis_size("row")
    emit = (lax.axis_index("col") + section[0]) % n_row
    tiles = positions.shape[1] // TILE
    packed = jnp.concatenate([positions, normals, areas[None], radiosity], 0)
    packed = from_root(packed, "row", emit)
    mask = lax.dynamic_slice_in_dim(visible, emit * tiles, tiles, 1)
    count, codes = visible_groups(mask)
    rec = receiver_features(positions, normals)
    em, emit_rows = emitter_features(packed[:3], packed[3:6], packed[6])
    rad = packed[7:]
    rad = rad.reshape(rad.shape[0], -1, TILE).transpose(1, 0, 2)
    rad = jnp.concatenate([rad, jnp.zeros_like(rad[:1])], 0)
    term = block_term(count, codes, rec, em, emit_rows, rad)
    return carried + reflect[None, :] * term


def solution(mesh):
    placed = (
        P(None, "row"),
        P(None, "row"),
        P("row"),
        P(None, "row"),
        P("row"),
        P("col", "row"),
        P("row", None),
        P(),
    )
    return jax.shard_map(
        on_device, mesh=mesh, in_specs=placed, out_specs=P("col", "row"), check_vma=False
    )
```

```python
import functools
import math

import jax
import jax.numpy as jnp
from jax import lax
from jax.experimental import pallas as pl
from jax.experimental.pallas import tpu as pltpu
from jax.sharding import PartitionSpec as P

BF = jnp.bfloat16
F32 = jnp.float32
TILE = 128
CHUNK = 16
FEATURES = 48
BITS = 6
STEP = 16
FROM_PRODUCT = (True, True, False)
KAPPA = (math.pi - 1) / (2 * math.pi)
SIGMA = (math.pi + 1) / (2 * math.pi)


def split3(x):
    high = lax.reduce_precision(x, 8, 7)
    rest = x - high
    mid = lax.reduce_precision(rest, 8, 7)
    return high.astype(BF), mid.astype(BF), (rest - mid).astype(BF)


def receiver_features(pos, nrm):
    p, n = pos.astype(F32), nrm.astype(F32)
    square = split3(p[0] * p[0] + p[1] * p[1] + p[2] * p[2])
    own = split3(-(n[0] * p[0] + n[1] * p[1] + n[2] * p[2]))
    one, zero = jnp.ones_like(pos[0]), jnp.zeros_like(pos[0])
    place, none = [pos[0], pos[1], pos[2]], [zero] * 3
    width = (place + none + [one, zero]) * 3
    width += [square[i] for i in (0, 1, 2, 0, 1, 0)] + [zero] * 18
    receive = [zero] * 30 + [own[0], own[1], nrm[0], nrm[1], nrm[2]]
    receive += [zero] * 4 + [own[2]] + [zero] * 8
    emit = (none + place + [zero, one]) * 3 + [zero] * 24
    f = jnp.stack(width + receive + emit, 0)
    f = f.reshape(3, FEATURES, -1, TILE // CHUNK, CHUNK).transpose(2, 3, 0, 4, 1)
    return f.reshape(-1, 3 * TILE, FEATURES)


def visible_pairs(mask):
    n_rec, n_em = mask.shape
    cum = jnp.cumsum(mask, axis=1)
    pairs = (cum[:, -1] + 1) // 2
    ends = jnp.cumsum(pairs)
    q = jnp.arange(n_rec * ((n_em + 1) // 2) + 2 * STEP, dtype=jnp.int32)
    a = jnp.sum((ends[None, :] <= q[:, None]).astype(jnp.int32), axis=1)
    hot = a[:, None] == jnp.arange(n_rec, dtype=jnp.int32)[None, :]
    rows = jnp.dot(hot.astype(F32), cum.astype(F32), preferred_element_type=F32)
    first = jnp.sum(jnp.where(hot, (ends - pairs)[None, :], 0), axis=1)
    rank = (2 * (q - first)).astype(F32)
    code = jnp.minimum(a, n_rec - 1)
    for t in range(2):
        code = (code << BITS) + jnp.sum((rows <= rank[:, None] + t).astype(jnp.int32), axis=1)
    return ends[-1:], code


def decoded(code):
    last = (1 << BITS) - 1
    return code >> (2 * BITS), [(code >> BITS) & last, code & last]


def lanes(tile):
    return pl.ds(pl.multiple_of(tile * TILE, TILE), TILE)


def rounded(x):
    return x.astype(BF).astype(F32)


def term_kernel(count, codes, rec, em, out, feat, rows, place, view):
    cases = out.shape[0]
    n_rec, n_em = rec.shape[0], em.shape[1] // TILE
    steps = (count[0] + STEP - 1) // STEP
    out[...] = jnp.zeros_like(out)
    view[...] = jnp.zeros_like(view)
    feat[:, n_em * TILE :] = jnp.zeros((FEATURES, TILE), BF)
    rows[:, n_em * TILE :] = jnp.zeros((8, TILE), F32)

    width = 4 * TILE if n_em % 4 == 0 else TILE

    def build(k, carry):
        at = pl.ds(pl.multiple_of(k * width, width), width)
        geo = em[cases:, at].astype(F32)
        row = lax.broadcasted_iota(jnp.int32, geo.shape, 0)
        px, py, pz, nx, ny, nz, area = (geo[i : i + 1] for i in range(7))
        scale = 1.0 / (KAPPA * area)
        main = geo * (scale * jnp.where(row < 3, -2.0, 1.0 / (math.pi * KAPPA)))
        middle = scale * (px * px + py * py + pz * pz) + SIGMA / KAPPA
        own = (nx * px + ny * py + nz * pz) * scale * (-1.0 / (math.pi * KAPPA))
        main = jnp.where(row < 6, main, jnp.where(row == 6, middle, own))
        high = rounded(main)
        mid = rounded(main - high)
        s_high = rounded(scale)
        s_mid = rounded(scale - s_high)
        s_low = scale - s_high - s_mid
        scales = jnp.where(row < 3, s_high, jnp.where(row < 5, s_mid, s_low))
        scales = jnp.where(row < 6, scales, 1.0)
        geo = jnp.where(row == 7, 1.0, geo)
        parts = [high, mid, main - high - mid, scales, geo, jnp.zeros_like(geo)]
        feat[:, at] = jnp.concatenate(parts, 0).astype(BF)
        rows[:, at] = main
        return carry

    lax.fori_loop(0, n_em * TILE // width, build, 0)

    def spread(a, carry):
        for k in range(TILE // CHUNK):
            at = pl.ds(k * CHUNK, CHUNK)
            place[a, at] = rec[a, 3 * k * CHUNK : (3 * k + 1) * CHUNK].astype(F32)
        return carry

    lax.fori_loop(0, n_rec, spread, 0, unroll=2)

    def views(a, tiles, slot):
        product_cos = FROM_PRODUCT[slot % len(FROM_PRODUCT)]
        kinds = 3 if product_cos else 2
        left = jnp.concatenate(
            [
                rec[a, 3 * r : 3 * r + kinds * CHUNK]
                for r in range(0, TILE, CHUNK)
            ],
            axis=0,
        )
        right = jnp.concatenate([feat[:, lanes(b)] for b in tiles], axis=1)
        products = jnp.dot(left, right, preferred_element_type=F32)
        emit = [rows[:, lanes(b)] for b in tiles]
        for r in range(0, TILE, CHUNK):
            if not product_cos:
                x, y, z = (
                    jnp.broadcast_to(place[a, r : r + CHUNK, k : k + 1], (CHUNK, TILE))
                    for k in range(3)
                )
            for t in range(2):
                m = products[kinds * r : kinds * (r + CHUNK), t * TILE : (t + 1) * TILE]
                if product_cos:
                    cos = m[2 * CHUNK :]
                else:
                    e = emit[t]
                    cos = e[3:4] * x + e[4:5] * y + e[5:6] * z + e[7:8]
                w = m[:CHUNK]
                v = jnp.maximum(cos, 0.0) * m[CHUNK : 2 * CHUNK]
                v = v * pltpu.reciprocal(w * w - 1.0, approx=True)
                at = slice(t * TILE, (t + 1) * TILE)
                view[slot, r : r + CHUNK, at] = jnp.maximum(v.astype(BF), 0)

    def add(a, tiles, slot):
        rad = jnp.concatenate([em[:cases, lanes(jnp.minimum(b, n_em - 1))] for b in tiles], axis=1)
        out[:, lanes(a)] += lax.dot_general(
            rad, view[slot], (((1,), (1,)), ((), ())), preferred_element_type=F32
        )

    def step(i, carry):
        for j in range(STEP):
            add(*decoded(codes[jnp.maximum(i - 1, 0) * STEP + j]), j)
            views(*decoded(codes[i * STEP + j]), j)
        return carry

    lax.fori_loop(0, steps + 1, step, 0)


def block_term(count, codes, rec, em, cases):
    tiles, columns = rec.shape[0], em.shape[1]
    smem = pl.BlockSpec(memory_space=pltpu.SMEM)
    vmem = pl.BlockSpec(memory_space=pltpu.VMEM)
    pairs = tiles * TILE * columns
    return pl.pallas_call(
        term_kernel,
        out_shape=jax.ShapeDtypeStruct((cases, tiles * TILE), F32),
        in_specs=[smem] * 2 + [vmem] * 2,
        out_specs=vmem,
        scratch_shapes=[
            pltpu.VMEM((FEATURES, columns + TILE), BF),
            pltpu.VMEM((8, columns + TILE), F32),
            pltpu.VMEM((tiles, TILE, FEATURES), F32),
            pltpu.VMEM((STEP, TILE, 2 * TILE), BF),
        ],
        compiler_params=pltpu.CompilerParams(vmem_limit_bytes=24 * 2**20),
        cost_estimate=pl.CostEstimate(
            flops=pairs * 300, bytes_accessed=8 * 2**20, transcendentals=pairs
        ),
        name="block_term",
    )(count, codes, rec, em)


def exchanged(block, axis, bits):
    return lax.ppermute(block, axis, [(i, i ^ bits) for i in range(lax.axis_size(axis))])


def from_root(block, axis, root):
    n = lax.axis_size(axis)
    away = lax.axis_index(axis) ^ root
    odd = lax.axis_index(axis) & 1
    half = block.shape[1] // 2
    block = jnp.where(away & 1 == 0, block, exchanged(block, axis, 1))
    mine = jnp.where(odd == 0, block[:, :half], block[:, half:])
    others = [mine] + [exchanged(mine, axis, bits) for bits in range(2, n, 2)]
    for k in range(1, n // 2):
        mine = jnp.where(away >> 1 == k, others[k], mine)
    other = exchanged(mine, axis, 1)
    parts = [jnp.where(odd == 0, mine, other), jnp.where(odd == 0, other, mine)]
    return jnp.concatenate(parts, axis=1)


def shifted(block, axis, distance):
    n = lax.axis_size(axis)
    return lax.ppermute(block, axis, [((i - distance) % n, i) for i in range(n)])


def on_device(positions, normals, areas, radiosity, reflect, partial_sums, visible, section):
    cases = radiosity.shape[0]
    n_row = lax.axis_size("row")
    emit = (lax.axis_index("col") + section[0]) % n_row
    tiles = positions.shape[1] // TILE
    packed = [radiosity, positions, normals, areas[None], jnp.zeros_like(areas)[None]]
    em = from_root(jnp.concatenate(packed, 0), "row", emit)
    carried = shifted(partial_sums, "col", 1)
    mask = lax.dynamic_slice_in_dim(visible, emit * tiles, tiles, 1)
    count, codes = visible_pairs(mask)
    rec = receiver_features(positions, normals)
    term = block_term(count, codes, rec, em, cases)
    return carried + reflect[None, :] * term


def solution(mesh):
    placed = (
        P(None, "row"),
        P(None, "row"),
        P("row"),
        P(None, "row"),
        P("row"),
        P("col", "row"),
        P("row", None),
        P(),
    )
    return jax.shard_map(
        on_device, mesh=mesh, in_specs=placed, out_specs=P("col", "row"), check_vma=False
    )
```

```python
import functools
import math

import jax
import jax.numpy as jnp
from jax import lax
from jax.experimental import pallas as pl
from jax.experimental.pallas import tpu as pltpu
from jax.sharding import PartitionSpec as P

BF = jnp.bfloat16
F32 = jnp.float32
TILE = 128
CHUNK = 16
FEATURES = 48
BITS = 6
STEP = 16
BUILD = 4
RECEIVE = 8
FROM_PRODUCT = (True, True, False)
KAPPA = (math.pi - 1) / (2 * math.pi)
SIGMA = (math.pi + 1) / (2 * math.pi)


def visible_pairs(mask):
    n_rec, n_em = mask.shape
    cum = jnp.cumsum(mask, axis=1)
    pairs = (cum[:, -1] + 1) // 2
    ends = jnp.cumsum(pairs)
    q = jnp.arange(n_rec * ((n_em + 1) // 2) + 2 * STEP, dtype=jnp.int32)
    a = jnp.sum((ends[None, :] <= q[:, None]).astype(jnp.int32), axis=1)
    hot = a[:, None] == jnp.arange(n_rec, dtype=jnp.int32)[None, :]
    rows = jnp.dot(hot.astype(F32), cum.astype(F32), preferred_element_type=F32)
    first = jnp.sum(jnp.where(hot, (ends - pairs)[None, :], 0), axis=1)
    rank = (2 * (q - first)).astype(F32)
    code = jnp.minimum(a, n_rec - 1)
    for t in range(2):
        code = (code << BITS) + jnp.sum((rows <= rank[:, None] + t).astype(jnp.int32), axis=1)
    return ends[-1:], code


def decoded(code):
    last = (1 << BITS) - 1
    return code >> (2 * BITS), [(code >> BITS) & last, code & last]


def lanes(tile):
    return pl.ds(pl.multiple_of(tile * TILE, TILE), TILE)


def rounded(x):
    return x.astype(BF).astype(F32)


def term_kernel(count, codes, own, *refs):
    pieces, (out, feat, rows, rad, rec, place, view) = refs[:-7], refs[-7:]
    cases = out.shape[0]
    n_rec, n_em = own.shape[1] // TILE, rad.shape[1] // TILE - 1
    steps = (count[0] + STEP - 1) // STEP
    out[...] = jnp.zeros_like(out)
    view[...] = jnp.zeros_like(view)
    feat[:, n_em * TILE :] = jnp.zeros((FEATURES, TILE), BF)
    rows[:, n_em * TILE :] = jnp.zeros((8, TILE), F32)
    rad[:, n_em * TILE :] = jnp.zeros((cases, TILE), BF)

    def build(piece, start, k):
        width = BUILD * TILE if piece.shape[1] % (BUILD * TILE) == 0 else TILE
        taken = pl.ds(pl.multiple_of(k * width, width), width)
        at = pl.ds(pl.multiple_of(start + k * width, TILE), width)
        rad[:, at] = piece[:cases, taken]
        geo = piece[cases:, taken].astype(F32)
        row = lax.broadcasted_iota(jnp.int32, geo.shape, 0)
        px, py, pz, nx, ny, nz, area = (geo[i : i + 1] for i in range(7))
        scale = 1.0 / (KAPPA * area)
        main = geo * (scale * jnp.where(row < 3, -2.0, 1.0 / (math.pi * KAPPA)))
        middle = scale * (px * px + py * py + pz * pz) + SIGMA / KAPPA
        own = (nx * px + ny * py + nz * pz) * scale * (-1.0 / (math.pi * KAPPA))
        main = jnp.where(row < 6, main, jnp.where(row == 6, middle, own))
        high = rounded(main)
        mid = rounded(main - high)
        s_high = rounded(scale)
        s_mid = rounded(scale - s_high)
        s_low = scale - s_high - s_mid
        scales = jnp.where(row < 3, s_high, jnp.where(row < 5, s_mid, s_low))
        scales = jnp.where(row < 6, scales, 1.0)
        geo = jnp.where(row == 7, 1.0, geo)
        parts = [high, mid, main - high - mid, scales, geo, jnp.zeros_like(geo)]
        feat[:, at] = jnp.concatenate(parts, 0).astype(BF)
        rows[:, at] = main

    start = 0
    for piece in pieces:
        columns = piece.shape[1]
        count_here = columns // (BUILD * TILE if columns % (BUILD * TILE) == 0 else TILE)

        def build_here(k, carry, piece=piece, start=start):
            build(piece, start, k)
            return carry

        lax.fori_loop(0, count_here, build_here, 0, unroll=True)
        start += columns

    turn = jnp.where(
        lax.broadcasted_iota(jnp.int32, (TILE, TILE), 0)
        == lax.broadcasted_iota(jnp.int32, (TILE, TILE), 1),
        1.0,
        0.0,
    ).astype(BF)

    def receive(a, carry):
        geo = own[:, lanes(a)].astype(F32)
        row = lax.broadcasted_iota(jnp.int32, geo.shape, 0)
        none = jnp.zeros_like(geo)
        px, py, pz, nx, ny, nz = (geo[i : i + 1] for i in range(6))
        square = px * px + py * py + pz * pz
        s_high = rounded(square)
        s_mid = rounded(square - s_high)
        s_low = square - s_high - s_mid
        back = -(nx * px + ny * py + nz * pz)
        b_high = rounded(back)
        b_mid = rounded(back - b_high)
        b_low = back - b_high - b_mid
        first = jnp.where(row < 3, geo, jnp.where(row == 6, 1.0, 0.0))
        second = jnp.where(row % 3 == 0, s_high, jnp.where(row % 3 == 1, s_mid, s_low))
        second = jnp.where(row < 5, second, jnp.where(row == 5, s_high, 0.0))
        wide = jnp.concatenate([first, first, first, second, none, none], 0)
        high = jnp.where(row == 6, b_high, jnp.where(row == 7, b_mid, 0.0))
        low = jnp.concatenate([nx, ny, nz] + [none[:4]] + [b_low], 0)
        facing = jnp.concatenate([none, none, none, high, low, none], 0)
        shift = jnp.concatenate([none[:3], px, py, pz, none[:1], none[:1] + 1.0], 0)
        lit = jnp.concatenate([shift, shift, shift, none, none, none], 0)
        for kind, f in enumerate((wide, facing, lit)):
            columns = lax.dot_general(
                turn, f.astype(BF), (((1,), (1,)), ((), ())), preferred_element_type=F32
            )
            if kind == 0:
                place[a] = columns
            columns = columns.astype(BF)
            for k in range(TILE // CHUNK):
                at = (3 * k + kind) * CHUNK
                rec[a, at : at + CHUNK] = columns[k * CHUNK : (k + 1) * CHUNK]
        return carry

    lax.fori_loop(0, n_rec, receive, 0, unroll=RECEIVE if n_rec % RECEIVE == 0 else 1)

    def views(a, tiles, slot):
        product_cos = FROM_PRODUCT[slot % len(FROM_PRODUCT)]
        kinds = 3 if product_cos else 2
        left = jnp.concatenate(
            [
                rec[a, 3 * r : 3 * r + kinds * CHUNK]
                for r in range(0, TILE, CHUNK)
            ],
            axis=0,
        )
        right = jnp.concatenate([feat[:, lanes(b)] for b in tiles], axis=1)
        products = jnp.dot(left, right, preferred_element_type=F32)
        emit = [rows[:, lanes(b)] for b in tiles]
        for r in range(0, TILE, CHUNK):
            if not product_cos:
                x, y, z = (
                    jnp.broadcast_to(place[a, r : r + CHUNK, k : k + 1], (CHUNK, TILE))
                    for k in range(3)
                )
            for t in range(2):
                m = products[kinds * r : kinds * (r + CHUNK), t * TILE : (t + 1) * TILE]
                if product_cos:
                    cos = m[2 * CHUNK :]
                else:
                    e = emit[t]
                    cos = e[3:4] * x + e[4:5] * y + e[5:6] * z + e[7:8]
                w = m[:CHUNK]
                v = jnp.maximum(cos, 0.0) * m[CHUNK : 2 * CHUNK]
                v = v * pltpu.reciprocal(w * w - 1.0, approx=True)
                at = slice(t * TILE, (t + 1) * TILE)
                view[slot, r : r + CHUNK, at] = jnp.maximum(v.astype(BF), 0)

    def add(a, tiles, slot):
        radiated = jnp.concatenate([rad[:, lanes(b)] for b in tiles], axis=1)
        out[:, lanes(a)] += lax.dot_general(
            radiated, view[slot], (((1,), (1,)), ((), ())), preferred_element_type=F32
        )

    def step(i, carry):
        for j in range(STEP):
            add(*decoded(codes[jnp.maximum(i - 1, 0) * STEP + j]), j)
            views(*decoded(codes[i * STEP + j]), j)
        return carry

    lax.fori_loop(0, steps, step, 0)
    for j in range(STEP):
        add(*decoded(codes[jnp.maximum(steps - 1, 0) * STEP + j]), j)


def block_term(count, codes, own, *pieces):
    cases = pieces[0].shape[0] - own.shape[0]
    columns = sum(piece.shape[1] for piece in pieces)
    tiles = own.shape[1] // TILE
    smem = pl.BlockSpec(memory_space=pltpu.SMEM)
    vmem = pl.BlockSpec(memory_space=pltpu.VMEM)
    pairs = tiles * TILE * columns
    return pl.pallas_call(
        term_kernel,
        out_shape=jax.ShapeDtypeStruct((cases, tiles * TILE), F32),
        in_specs=[smem] * 2 + [vmem] * (1 + len(pieces)),
        out_specs=vmem,
        scratch_shapes=[
            pltpu.VMEM((FEATURES, columns + TILE), BF),
            pltpu.VMEM((8, columns + TILE), F32),
            pltpu.VMEM((cases, columns + TILE), BF),
            pltpu.VMEM((tiles, 3 * TILE, FEATURES), BF),
            pltpu.VMEM((tiles, TILE, FEATURES), F32),
            pltpu.VMEM((STEP, TILE, 2 * TILE), BF),
        ],
        compiler_params=pltpu.CompilerParams(vmem_limit_bytes=24 * 2**20),
        cost_estimate=pl.CostEstimate(
            flops=pairs * 300, bytes_accessed=8 * 2**20, transcendentals=pairs
        ),
        name="block_term",
    )(count, codes, own, *pieces)


def exchanged(block, axis, bits):
    return lax.ppermute(block, axis, [(i, i ^ bits) for i in range(lax.axis_size(axis))])


def spread_from(root, axis, wide, narrow):
    n = lax.axis_size(axis)
    me = lax.axis_index(axis)
    away, odd = me ^ root, me & 1
    wide = jnp.where(away & 1 == 0, wide, exchanged(wide, axis, 1))
    narrow = jnp.where(away & 1 == 0, narrow, exchanged(narrow, axis, 1))
    block = jnp.concatenate([wide, narrow], 0)
    q = block.shape[1] // 4
    parts = [
        jnp.where(odd == 0, block[:, i * q : (i + 1) * q], block[:, (i + 2) * q : (i + 3) * q])
        for i in range(2)
    ]
    bits = [1 << i for i in range(1, n.bit_length() - 1)]
    for pair in zip(bits, bits[::-1]):
        got = [exchanged(part, axis, bit) for part, bit in zip(parts, pair)]
        parts = [jnp.where(away & bit == 0, x, y) for x, y, bit in zip(parts, got, pair)]
    mine = jnp.concatenate(parts, axis=1)
    return mine, exchanged(mine, axis, 1)


def shifted(block, axis, distance):
    n = lax.axis_size(axis)
    return lax.ppermute(block, axis, [((i - distance) % n, i) for i in range(n)])


def on_device(positions, normals, areas, radiosity, reflect, partial_sums, visible, section):
    n_row = lax.axis_size("row")
    emit = (lax.axis_index("col") + section[0]) % n_row
    tiles = positions.shape[1] // TILE
    own = jnp.concatenate([positions, normals, areas[None], areas[None]], 0)
    pieces = spread_from(emit, "row", radiosity, own)
    carried = shifted(partial_sums, "col", 1)
    mask = lax.dynamic_slice_in_dim(visible, emit * tiles, tiles, 1)
    half = tiles // 2
    swapped = jnp.concatenate([mask[:, half:], mask[:, :half]], 1)
    mask = jnp.where(lax.axis_index("row") & 1 == 0, mask, swapped)
    count, codes = visible_pairs(mask)
    return carried + reflect[None, :] * block_term(count, codes, own, *pieces)


def solution(mesh):
    placed = (
        P(None, "row"),
        P(None, "row"),
        P("row"),
        P(None, "row"),
        P("row"),
        P("col", "row"),
        P("row", None),
        P(),
    )
    return jax.shard_map(
        on_device, mesh=mesh, in_specs=placed, out_specs=P("col", "row"), check_vma=False
    )
```

```python
import functools
import math

import jax
import jax.numpy as jnp
from jax import lax
from jax.experimental import pallas as pl
from jax.experimental.pallas import tpu as pltpu
from jax.sharding import PartitionSpec as P

BF = jnp.bfloat16
F32 = jnp.float32
TILE = 128
CHUNK = 16
FEATURES = 48
BITS = 6
STEP = 24
BUILD = 4
UNROLL = 24
FROM_PRODUCT = (True, True, False)
KAPPA = (math.pi - 1) / (2 * math.pi)
SIGMA = (math.pi + 1) / (2 * math.pi)


def visible_pairs(mask):
    n_rec, n_em = mask.shape
    cum = jnp.cumsum(mask.T, axis=1)
    pairs = (cum[:, -1] + 1) // 2
    ends = jnp.cumsum(pairs)
    q = jnp.arange(n_em * ((n_rec + 1) // 2) + 2 * STEP, dtype=jnp.int32)
    b = jnp.sum((ends[None, :] <= q[:, None]).astype(jnp.int32), axis=1)
    hot = b[:, None] == jnp.arange(n_em, dtype=jnp.int32)[None, :]
    rows = jnp.dot(hot.astype(F32), cum.astype(F32), preferred_element_type=F32)
    first = jnp.sum(jnp.where(hot, (ends - pairs)[None, :], 0), axis=1)
    rank = (2 * (q - first)).astype(F32)
    code = jnp.minimum(b, n_em - 1)
    for t in range(2):
        code = (code << BITS) + jnp.sum((rows <= rank[:, None] + t).astype(jnp.int32), axis=1)
    return ends[-1:], code


def decoded(code):
    last = (1 << BITS) - 1
    return code >> (2 * BITS), [(code >> BITS) & last, code & last]


def lanes(tile):
    return pl.ds(pl.multiple_of(tile * TILE, TILE), TILE)


def rounded(x):
    return x.astype(BF).astype(F32)


def term_kernel(count, codes, own, *refs):
    pieces, (out, feat, rows, rad, em, place, view) = refs[:-7], refs[-7:]
    cases = out.shape[0]
    n_rec, n_em = own.shape[1] // TILE, rad.shape[1] // TILE
    steps = (count[0] + STEP - 1) // STEP
    out[...] = jnp.zeros_like(out)
    view[...] = jnp.zeros_like(view)
    feat[:, n_rec * TILE :] = jnp.zeros((FEATURES, TILE), BF)
    rows[:, n_rec * TILE :] = jnp.zeros((8, TILE), F32)

    width = BUILD * TILE if n_rec % BUILD == 0 else TILE

    def receivers(k, carry):
        at = pl.ds(pl.multiple_of(k * width, width), width)
        geo = own[:, at].astype(F32)
        row = lax.broadcasted_iota(jnp.int32, geo.shape, 0)
        px, py, pz, nx, ny, nz = (geo[i : i + 1] for i in range(6))
        square = px * px + py * py + pz * pz
        back = -(nx * px + ny * py + nz * pz)
        full = jnp.where(row < 3, square, back)
        high = rounded(full)
        mid = rounded(full - high)
        low = full - high - mid
        parts = jnp.where(row % 3 == 0, high, jnp.where(row % 3 == 1, mid, low))
        parts = jnp.where(row < 6, parts, 0.0)
        plain = jnp.where(row < 6, geo, jnp.where(row == 6, 1.0, 0.0))
        feat[:, at] = jnp.concatenate([plain] * 3 + [parts] * 3, 0).astype(BF)
        rows[:, at] = jnp.where(row == 6, back, plain)
        return carry

    lax.fori_loop(0, n_rec * TILE // width, receivers, 0, unroll=True)

    turn = jnp.where(
        lax.broadcasted_iota(jnp.int32, (TILE, TILE), 0)
        == lax.broadcasted_iota(jnp.int32, (TILE, TILE), 1),
        1.0,
        0.0,
    ).astype(BF)

    def emitters(piece, start, b):
        rad[:, lanes(start + b)] = piece[:cases, lanes(b)]
        geo = piece[cases:, lanes(b)].astype(F32)
        row = lax.broadcasted_iota(jnp.int32, geo.shape, 0)
        none = jnp.zeros_like(geo)
        px, py, pz, nx, ny, nz, area = (geo[i : i + 1] for i in range(7))
        scale = 1.0 / (KAPPA * area)
        main = geo * (scale * jnp.where(row < 3, -2.0, 1.0 / (math.pi * KAPPA)))
        middle = scale * (px * px + py * py + pz * pz) + SIGMA / KAPPA
        behind = (nx * px + ny * py + nz * pz) * scale * (-1.0 / (math.pi * KAPPA))
        main = jnp.where(row < 6, main, jnp.where(row == 6, middle, behind))
        high = rounded(main)
        mid = rounded(main - high)
        thirds = [high, mid, main - high - mid]
        s_high = rounded(scale)
        s_mid = rounded(scale - s_high)
        s_low = scale - s_high - s_mid
        w_row = (row < 3) | (row == 6)
        wide = [jnp.where(w_row, x, 0.0) for x in thirds]
        wide += [jnp.where(row < 3 - i, x, 0.0) for i, x in enumerate((s_high, s_mid, s_low))]
        lit = [
            jnp.concatenate([x[3:6], none[:3], x[7:8], none[:1]], 0) for x in thirds
        ] + [none] * 3
        spot = jnp.concatenate([none[:3], px, py, pz, none[:2]], 0)
        ones = jnp.where((row >= 3) & (row < 6), 1.0, 0.0)
        facing = [spot, none, none, ones, none, none]
        for kind, f in enumerate((wide, lit, facing)):
            f = jnp.concatenate(f, 0).astype(BF)
            columns = lax.dot_general(
                turn, f, (((1,), (1,)), ((), ())), preferred_element_type=F32
            )
            if kind == 2:
                place[start + b] = columns
            columns = columns.astype(BF)
            for k in range(TILE // CHUNK):
                at = (3 * k + kind) * CHUNK
                em[start + b, at : at + CHUNK] = columns[k * CHUNK : (k + 1) * CHUNK]

    start = 0
    for piece in pieces:
        tiles_here = piece.shape[1] // TILE

        def emitters_here(b, carry, piece=piece, start=start):
            emitters(piece, start, b)
            return carry

        unroll = UNROLL if tiles_here % UNROLL == 0 else 1
        lax.fori_loop(0, tiles_here, emitters_here, 0, unroll=unroll)
        start += tiles_here

    def kinds_of(slot):
        return 3 if FROM_PRODUCT[slot % len(FROM_PRODUCT)] else 2

    def products_of(b, tiles, slot):
        rows_taken = kinds_of(slot) * CHUNK
        left = jnp.concatenate(
            [em[b, 3 * r : 3 * r + rows_taken] for r in range(0, TILE, CHUNK)], axis=0
        )
        right = jnp.concatenate([feat[:, lanes(a)] for a in tiles], axis=1)
        return jnp.dot(left, right, preferred_element_type=F32)

    def views(products, b, tiles, slot):
        kinds = kinds_of(slot)
        from_product = kinds == 3
        receive = [rows[:, lanes(a)] for a in tiles]
        for r in range(0, TILE, CHUNK):
            if not from_product:
                x, y, z = (
                    jnp.broadcast_to(place[b, r : r + CHUNK, k : k + 1], (CHUNK, TILE))
                    for k in range(3, 6)
                )
            for t in range(2):
                m = products[kinds * r : kinds * (r + CHUNK), t * TILE : (t + 1) * TILE]
                if from_product:
                    cos = m[2 * CHUNK :]
                else:
                    n = receive[t]
                    cos = n[3:4] * x + n[4:5] * y + n[5:6] * z + n[6:7]
                w = m[:CHUNK]
                v = jnp.maximum(cos, 0.0) * m[CHUNK : 2 * CHUNK]
                v = v * pltpu.reciprocal(w * w - 1.0, approx=True)
                at = slice(t * TILE, (t + 1) * TILE)
                view[slot, r : r + CHUNK, at] = jnp.maximum(v.astype(BF), 0)

    def add(b, tiles, slot):
        total = jnp.dot(rad[:, lanes(b)], view[slot], preferred_element_type=F32)
        for t, a in enumerate(tiles):
            out[:, lanes(jnp.minimum(a, n_rec - 1))] += total[:, t * TILE : (t + 1) * TILE]

    def step(i, carry):
        for j in range(STEP):
            add(*decoded(codes[jnp.maximum(i - 1, 0) * STEP + j]), j)
            tiles = decoded(codes[i * STEP + j])
            views(products_of(*tiles, j), *tiles, j)
        return carry

    lax.fori_loop(0, steps, step, 0)
    for j in range(STEP):
        add(*decoded(codes[jnp.maximum(steps - 1, 0) * STEP + j]), j)


def block_term(count, codes, own, *pieces):
    cases = pieces[0].shape[0] - own.shape[0]
    columns = sum(piece.shape[1] for piece in pieces)
    tiles = own.shape[1] // TILE
    smem = pl.BlockSpec(memory_space=pltpu.SMEM)
    vmem = pl.BlockSpec(memory_space=pltpu.VMEM)
    pairs = tiles * TILE * columns
    return pl.pallas_call(
        term_kernel,
        out_shape=jax.ShapeDtypeStruct((cases, tiles * TILE), F32),
        in_specs=[smem] * 2 + [vmem] * (1 + len(pieces)),
        out_specs=vmem,
        scratch_shapes=[
            pltpu.VMEM((FEATURES, (tiles + 1) * TILE), BF),
            pltpu.VMEM((8, (tiles + 1) * TILE), F32),
            pltpu.VMEM((cases, columns), BF),
            pltpu.VMEM((columns // TILE, 3 * TILE, FEATURES), BF),
            pltpu.VMEM((columns // TILE, TILE, FEATURES), F32),
            pltpu.VMEM((STEP, TILE, 2 * TILE), BF),
        ],
        compiler_params=pltpu.CompilerParams(vmem_limit_bytes=24 * 2**20),
        cost_estimate=pl.CostEstimate(
            flops=pairs * 300, bytes_accessed=8 * 2**20, transcendentals=pairs
        ),
        name="block_term",
    )(count, codes, own, *pieces)


def exchanged(block, axis, bits):
    return lax.ppermute(block, axis, [(i, i ^ bits) for i in range(lax.axis_size(axis))])


def spread_from(root, axis, wide, narrow):
    n = lax.axis_size(axis)
    me = lax.axis_index(axis)
    away, odd = me ^ root, me & 1
    wide = jnp.where(away & 1 == 0, wide, exchanged(wide, axis, 1))
    narrow = jnp.where(away & 1 == 0, narrow, exchanged(narrow, axis, 1))
    block = jnp.concatenate([wide, narrow], 0)
    q = block.shape[1] // 4
    parts = [
        jnp.where(odd == 0, block[:, i * q : (i + 1) * q], block[:, (i + 2) * q : (i + 3) * q])
        for i in range(2)
    ]
    bits = [1 << i for i in range(1, n.bit_length() - 1)]
    for pair in zip(bits, bits[::-1]):
        got = [exchanged(part, axis, bit) for part, bit in zip(parts, pair)]
        parts = [jnp.where(away & bit == 0, x, y) for x, y, bit in zip(parts, got, pair)]
    mine = jnp.concatenate(parts, axis=1)
    return mine, exchanged(mine, axis, 1)


def shifted(block, axis, distance):
    n = lax.axis_size(axis)
    return lax.ppermute(block, axis, [((i - distance) % n, i) for i in range(n)])


def on_device(positions, normals, areas, radiosity, reflect, partial_sums, visible, section):
    n_row = lax.axis_size("row")
    emit = (lax.axis_index("col") + section[0]) % n_row
    tiles = positions.shape[1] // TILE
    own = jnp.concatenate([positions, normals, areas[None], areas[None]], 0)
    pieces = spread_from(emit, "row", radiosity, own)
    carried = shifted(partial_sums, "col", 1)
    mask = lax.dynamic_slice_in_dim(visible, emit * tiles, tiles, 1)
    half = tiles // 2
    swapped = jnp.concatenate([mask[:, half:], mask[:, :half]], 1)
    mask = jnp.where(lax.axis_index("row") & 1 == 0, mask, swapped)
    count, codes = visible_pairs(mask)
    return carried + reflect[None, :] * block_term(count, codes, own, *pieces)


def solution(mesh):
    placed = (
        P(None, "row"),
        P(None, "row"),
        P("row"),
        P(None, "row"),
        P("row"),
        P("col", "row"),
        P("row", None),
        P(),
    )
    return jax.shard_map(
        on_device, mesh=mesh, in_specs=placed, out_specs=P("col", "row"), check_vma=False
    )
```

```python
import functools
import math

import jax
import jax.numpy as jnp
from jax import lax
from jax.experimental import pallas as pl
from jax.experimental.pallas import tpu as pltpu
from jax.sharding import PartitionSpec as P

BF = jnp.bfloat16
F32 = jnp.float32
TILE = 128
CHUNK = 16
FEATURES = 48
BITS = 6
STEP = 24
BUILD = 4
UNROLL = 24
FROM_PRODUCT = (True, True, False)
KAPPA = (math.pi - 1) / (2 * math.pi)
SIGMA = (math.pi + 1) / (2 * math.pi)


def visible_pairs(mask):
    n_rec, n_em = mask.shape
    cum = jnp.cumsum(mask.T, axis=1)
    pairs = (cum[:, -1] + 1) // 2
    ends = jnp.cumsum(pairs)
    q = jnp.arange(n_em * ((n_rec + 1) // 2) + 2 * STEP, dtype=jnp.int32)
    b = jnp.sum((ends[None, :] <= q[:, None]).astype(jnp.int32), axis=1)
    hot = b[:, None] == jnp.arange(n_em, dtype=jnp.int32)[None, :]
    rows = jnp.dot(hot.astype(F32), cum.astype(F32), preferred_element_type=F32)
    first = jnp.sum(jnp.where(hot, (ends - pairs)[None, :], 0), axis=1)
    rank = (2 * (q - first)).astype(F32)
    code = jnp.minimum(b, n_em - 1)
    for t in range(2):
        code = (code << BITS) + jnp.sum((rows <= rank[:, None] + t).astype(jnp.int32), axis=1)
    return ends, code


def decoded(code):
    last = (1 << BITS) - 1
    return code >> (2 * BITS), [(code >> BITS) & last, code & last]


def lanes(tile):
    return pl.ds(pl.multiple_of(tile * TILE, TILE), TILE)


def rounded(x):
    return x.astype(BF).astype(F32)


def term_kernel(ends, codes, own, *refs):
    pieces, (out, feat, rows, rad, em, place, view) = refs[:-7], refs[-7:]
    cases = out.shape[0]
    n_rec, n_em = own.shape[1] // TILE, rad.shape[1] // TILE
    steps = (ends[n_em - 1] + STEP - 1) // STEP
    out[...] = jnp.zeros_like(out)
    view[...] = jnp.zeros_like(view)
    feat[:, n_rec * TILE :] = jnp.zeros((FEATURES, TILE), BF)
    rows[:, n_rec * TILE :] = jnp.zeros((8, TILE), F32)

    width = BUILD * TILE if n_rec % BUILD == 0 else TILE

    def receivers(k, carry):
        at = pl.ds(pl.multiple_of(k * width, width), width)
        geo = own[:, at].astype(F32)
        row = lax.broadcasted_iota(jnp.int32, geo.shape, 0)
        px, py, pz, nx, ny, nz = (geo[i : i + 1] for i in range(6))
        square = px * px + py * py + pz * pz
        back = -(nx * px + ny * py + nz * pz)
        full = jnp.where(row < 3, square, back)
        high = rounded(full)
        mid = rounded(full - high)
        low = full - high - mid
        parts = jnp.where(row % 3 == 0, high, jnp.where(row % 3 == 1, mid, low))
        parts = jnp.where(row < 6, parts, 0.0)
        plain = jnp.where(row < 6, geo, jnp.where(row == 6, 1.0, 0.0))
        feat[:, at] = jnp.concatenate([plain] * 3 + [parts] * 3, 0).astype(BF)
        rows[:, at] = jnp.where(row == 6, back, plain)
        return carry

    lax.fori_loop(0, n_rec * TILE // width, receivers, 0, unroll=True)

    turn = jnp.where(
        lax.broadcasted_iota(jnp.int32, (TILE, TILE), 0)
        == lax.broadcasted_iota(jnp.int32, (TILE, TILE), 1),
        1.0,
        0.0,
    ).astype(BF)

    def emitters(piece, start, b):
        rad[:, lanes(start + b)] = piece[:cases, lanes(b)]
        geo = piece[cases:, lanes(b)].astype(F32)
        row = lax.broadcasted_iota(jnp.int32, geo.shape, 0)
        none = jnp.zeros_like(geo)
        px, py, pz, nx, ny, nz, area = (geo[i : i + 1] for i in range(7))
        scale = 1.0 / (KAPPA * area)
        main = geo * (scale * jnp.where(row < 3, -2.0, 1.0 / (math.pi * KAPPA)))
        middle = scale * (px * px + py * py + pz * pz) + SIGMA / KAPPA
        behind = (nx * px + ny * py + nz * pz) * scale * (-1.0 / (math.pi * KAPPA))
        main = jnp.where(row < 6, main, jnp.where(row == 6, middle, behind))
        high = rounded(main)
        mid = rounded(main - high)
        thirds = [high, mid, main - high - mid]
        s_high = rounded(scale)
        s_mid = rounded(scale - s_high)
        s_low = scale - s_high - s_mid
        w_row = (row < 3) | (row == 6)
        wide = [jnp.where(w_row, x, 0.0) for x in thirds]
        wide += [jnp.where(row < 3 - i, x, 0.0) for i, x in enumerate((s_high, s_mid, s_low))]
        lit = [
            jnp.concatenate([x[3:6], none[:3], x[7:8], none[:1]], 0) for x in thirds
        ] + [none] * 3
        spot = jnp.concatenate([none[:3], px, py, pz, none[:2]], 0)
        ones = jnp.where((row >= 3) & (row < 6), 1.0, 0.0)
        facing = [spot, none, none, ones, none, none]
        f = jnp.concatenate([*wide, none, none, *lit, none, none, *facing], 0).astype(BF)
        columns = lax.dot_general(
            turn, f, (((1,), (1,)), ((), ())), preferred_element_type=F32
        )
        kinds = [columns[:, :TILE], pltpu.roll(columns[:, :TILE], TILE // 2, 1), columns[:, TILE:]]
        place[start + b] = kinds[2][:, :FEATURES]
        for kind, columns in enumerate(kinds):
            columns = columns[:, :FEATURES].astype(BF)
            for k in range(TILE // CHUNK):
                at = (3 * k + kind) * CHUNK
                em[start + b, at : at + CHUNK] = columns[k * CHUNK : (k + 1) * CHUNK]

    start = 0
    for piece in pieces:
        tiles_here = piece.shape[1] // TILE

        def emitters_here(b, carry, piece=piece, start=start):
            emitters(piece, start, b)
            return carry

        unroll = UNROLL if tiles_here % UNROLL == 0 else 1
        lax.fori_loop(0, tiles_here, emitters_here, 0, unroll=unroll)
        start += tiles_here

    def kinds_of(slot):
        return 3 if FROM_PRODUCT[slot % len(FROM_PRODUCT)] else 2

    def products_of(b, tiles, slot):
        rows_taken = kinds_of(slot) * CHUNK
        left = jnp.concatenate(
            [em[b, 3 * r : 3 * r + rows_taken] for r in range(0, TILE, CHUNK)], axis=0
        )
        right = jnp.concatenate([feat[:, lanes(a)] for a in tiles], axis=1)
        return jnp.dot(left, right, preferred_element_type=F32)

    def views(products, b, tiles, slot):
        kinds = kinds_of(slot)
        from_product = kinds == 3
        receive = [rows[:, lanes(a)] for a in tiles]
        for r in range(0, TILE, CHUNK):
            if not from_product:
                x, y, z = (
                    jnp.broadcast_to(place[b, r : r + CHUNK, k : k + 1], (CHUNK, TILE))
                    for k in range(3, 6)
                )
            for t in range(2):
                m = products[kinds * r : kinds * (r + CHUNK), t * TILE : (t + 1) * TILE]
                if from_product:
                    cos = m[2 * CHUNK :]
                else:
                    n = receive[t]
                    cos = n[3:4] * x + n[4:5] * y + n[5:6] * z + n[6:7]
                w = m[:CHUNK]
                v = jnp.maximum(cos, 0.0) * m[CHUNK : 2 * CHUNK]
                v = v * pltpu.reciprocal(w * w - 1.0, approx=True)
                at = slice(t * TILE, (t + 1) * TILE)
                view[slot, r : r + CHUNK, at] = jnp.maximum(v.astype(BF), 0)

    def add(b, tiles, slot):
        total = jnp.dot(rad[:, lanes(b)], view[slot], preferred_element_type=F32)
        for t, a in enumerate(tiles):
            out[:, lanes(jnp.minimum(a, n_rec - 1))] += total[:, t * TILE : (t + 1) * TILE]

    def step(i, carry):
        for j in range(STEP):
            add(*decoded(codes[jnp.maximum(i - 1, 0) * STEP + j]), j)
            tiles = decoded(codes[i * STEP + j])
            views(products_of(*tiles, j), *tiles, j)
        return carry

    lax.fori_loop(0, steps, step, 0)
    for j in range(STEP):
        add(*decoded(codes[jnp.maximum(steps - 1, 0) * STEP + j]), j)


def block_term(ends, codes, own, *pieces):
    cases = pieces[0].shape[0] - own.shape[0]
    columns = sum(piece.shape[1] for piece in pieces)
    tiles = own.shape[1] // TILE
    smem = pl.BlockSpec(memory_space=pltpu.SMEM)
    vmem = pl.BlockSpec(memory_space=pltpu.VMEM)
    pairs = tiles * TILE * columns
    return pl.pallas_call(
        term_kernel,
        out_shape=jax.ShapeDtypeStruct((cases, tiles * TILE), F32),
        in_specs=[smem] * 2 + [vmem] * (1 + len(pieces)),
        out_specs=vmem,
        scratch_shapes=[
            pltpu.VMEM((FEATURES, (tiles + 1) * TILE), BF),
            pltpu.VMEM((8, (tiles + 1) * TILE), F32),
            pltpu.VMEM((cases, columns), BF),
            pltpu.VMEM((columns // TILE, 3 * TILE, FEATURES), BF),
            pltpu.VMEM((columns // TILE, TILE, FEATURES), F32),
            pltpu.VMEM((STEP, TILE, 2 * TILE), BF),
        ],
        compiler_params=pltpu.CompilerParams(vmem_limit_bytes=24 * 2**20),
        cost_estimate=pl.CostEstimate(
            flops=pairs * 300, bytes_accessed=8 * 2**20, transcendentals=pairs
        ),
        name="block_term",
    )(ends, codes, own, *pieces)


def exchanged(block, axis, bits):
    return lax.ppermute(block, axis, [(i, i ^ bits) for i in range(lax.axis_size(axis))])


def spread_from(root, axis, wide, narrow, later):
    n = lax.axis_size(axis)
    me = lax.axis_index(axis)
    away, odd = me ^ root, me & 1
    wide = jnp.where(away & 1 == 0, wide, exchanged(wide, axis, 1))
    narrow = jnp.where(away & 1 == 0, narrow, exchanged(narrow, axis, 1))
    block = jnp.concatenate([wide, narrow], 0)
    q = block.shape[1] // 4
    parts = [
        jnp.where(odd == 0, block[:, i * q : (i + 1) * q], block[:, (i + 2) * q : (i + 3) * q])
        for i in range(2)
    ]
    bits = [1 << i for i in range(1, n.bit_length() - 1)]
    for pair in zip(bits, bits[::-1]):
        got = [exchanged(part, axis, bit) for part, bit in zip(parts, pair)]
        parts = [jnp.where(away & bit == 0, x, y) for x, y, bit in zip(parts, got, pair)]
        if pair[0] == bits[0]:
            parts, later = lax.optimization_barrier((parts, later))
    mine = jnp.concatenate(parts, axis=1)
    return (mine, exchanged(mine, axis, 1)), later


def shifted(block, axis, distance):
    n = lax.axis_size(axis)
    return lax.ppermute(block, axis, [((i - distance) % n, i) for i in range(n)])


def on_device(positions, normals, areas, radiosity, reflect, partial_sums, visible, section):
    n_row = lax.axis_size("row")
    emit = (lax.axis_index("col") + section[0]) % n_row
    tiles = positions.shape[1] // TILE
    own = jnp.concatenate([positions, normals, areas[None], areas[None]], 0)
    mask = lax.dynamic_slice_in_dim(visible, emit * tiles, tiles, 1)
    half = tiles // 2
    swapped = jnp.concatenate([mask[:, half:], mask[:, :half]], 1)
    mask = jnp.where(lax.axis_index("row") & 1 == 0, mask, swapped)
    ends, codes = visible_pairs(mask)
    later = (partial_sums, ends, codes)
    pieces, (partial_sums, ends, codes) = spread_from(emit, "row", radiosity, own, later)
    carried = shifted(partial_sums, "col", 1)
    return carried + reflect[None, :] * block_term(ends, codes, own, *pieces)


def solution(mesh):
    placed = (
        P(None, "row"),
        P(None, "row"),
        P("row"),
        P(None, "row"),
        P("row"),
        P("col", "row"),
        P("row", None),
        P(),
    )
    return jax.shard_map(
        on_device, mesh=mesh, in_specs=placed, out_specs=P("col", "row"), check_vma=False
    )
```
